512 devices in a mesh: row: 16 (over x, y_hi, core), col: 32 (over y_lo, z).
Axes of the slice: x: 4, y: 8 (y_hi: 2, y_lo: 4; y = y_hi * 4 + y_lo), z: 8, core: 2. Of those that a mesh axis runs over, the one named last changes fastest.
Arguments:
- vectors: bfloat16 [16, 524288], P(None, ('row', 'col')), may hold values from -6 to 6
- tiles: bfloat16 [16, 32, 8, 512, 512], P('row', 'col'), may hold values from -0.25 to 0.25
- block_rows: int32 [16, 32, 8], P('row', 'col'), may hold values from 0 to 63
- block_cols: int32 [16, 32, 8], P('row', 'col'), may hold values from 0 to 31
- counts: int32 [16, 32], P('row', 'col'), may hold values from 1 to 8, as said below
Outputs:
- hx: float32 [16, 524288], P(None, ('row', 'col'))
The draws below stay inside these ranges and needn't reach their ends.
Inputs may be any that keep to these rules, and one draw needn't show every extreme that they name: `counts`: every tile has between 1 and 8 live blocks; in every draw one tile has all 8 slots live, the others at most half.
All inputs are finite; a program needn't handle non-finite values.
Results may differ from the reference program's by a relative error of at most 0.0003.
Values may be sent and summed in bfloat16 or wider, within the bound.
A program may use at most 64 MiB of HBM per device.

```python
import jax
import jax.numpy as jnp
from jax import lax

VECS = 16
BLK = 512
BD = 2
NNZ_DEV = 8
ROWS = 524288
N_ROW = 16
N_COL = 32


def draw_counts(key, part):
    key = jax.random.fold_in(key, 7)
    first, second = jax.random.split(key)
    total = N_ROW * N_COL
    base = jax.random.randint(first, (total,), 1, NNZ_DEV // 2 + 1)
    chosen = jax.random.randint(second, (), 0, total)
    base = jnp.where(jnp.arange(total) == chosen, NNZ_DEV, base)
    return base.reshape(N_ROW, N_COL).astype(jnp.int32)


def plant(values, key, smallest, top_value):
    longest = values.shape.index(max(values.shape))
    spots = []
    for shift in (0, 1):
        where = [jax.random.randint(jax.random.fold_in(key, axis), (), 0, length) for axis, length in enumerate(values.shape)]
        where[longest] = (where[longest] + shift) % values.shape[longest]
        spots.append(tuple(where))
    return values.at[spots[0]].set(smallest).at[spots[1]].set(top_value)


def levels(key, dims, shards, smallest, high):
    def one(dim, shards_of):
        steps = jax.random.uniform(jax.random.fold_in(jax.random.fold_in(key, 6), dim), (shards_of,), jnp.float32, smallest / len(shards), high / len(shards))
        return jnp.repeat(jnp.exp(steps), dims[dim] // shards_of).reshape((-1,) + (1,) * (len(dims) - dim - 1))

    factor_of = one(*shards[0])
    for cut in shards[1:]:
        factor_of = factor_of * one(*cut)
    return factor_of


def centred(stream_key, extent, scale, most, pieces=(), held_as=jnp.bfloat16):
    values = jax.random.normal(stream_key, extent, jnp.float32) * scale
    if len(pieces) > 0:
        values = levels(stream_key, extent, pieces, -0.22, 0.18) * values
    return jnp.clip(values, min=-most, max=most).astype(held_as)


def setup_inputs(seed: int = 0) -> dict:
    seeds = jax.random.split(jax.random.key(seed), 6)
    vectors = centred(seeds[0], (VECS, ROWS), 1.0, 6.0, ((1, 512),))
    tiles = centred(seeds[1], (N_ROW, N_COL, NNZ_DEV, BLK, BLK), BLK ** -0.5, 0.25, ((0, 16), (1, 32)))
    block_rows = plant(jax.random.randint(seeds[2], (N_ROW, N_COL, NNZ_DEV), 0, N_COL * BD), jax.random.fold_in(seeds[2], 1), 0, (N_COL * BD) - 1).astype(jnp.int32)
    block_cols = plant(jax.random.randint(seeds[3], (N_ROW, N_COL, NNZ_DEV), 0, N_ROW * BD), jax.random.fold_in(seeds[3], 1), 0, (N_ROW * BD) - 1).astype(jnp.int32)
    counts = draw_counts(jax.random.fold_in(seeds[5], 71), 0)
    return dict(vectors=vectors, tiles=tiles, block_rows=block_rows, block_cols=block_cols, counts=counts)


def add_at(total, piece, start):
    width = piece.shape[1]
    old = lax.dynamic_slice_in_dim(total, start, width, 1)
    return lax.dynamic_update_slice_in_dim(total, old + piece, start, 1)


def reference(vectors, tiles, block_rows, block_cols, counts):
    block_size = tiles.shape[-1]
    group = N_COL * BD
    flat_tiles = tiles.reshape(N_ROW * N_COL * NNZ_DEV, block_size, block_size)
    row_ids = jnp.arange(N_ROW, dtype=jnp.int32)[:, None, None]
    col_ids = jnp.arange(N_COL, dtype=jnp.int32)[None, :, None]
    slot_ids = jnp.arange(NNZ_DEV, dtype=jnp.int32)[None, None, :]
    global_rows = (row_ids * group + block_rows).astype(jnp.int32).reshape(-1)
    global_cols = ((block_cols // BD) * group + col_ids * BD + block_cols % BD).astype(jnp.int32).reshape(-1)
    live = (slot_ids < counts[:, :, None]).reshape(-1)

    def apply_block(result, items):
        block, row_block, col_block, alive = items
        row_start = (row_block * block_size).astype(jnp.int32)
        col_start = (col_block * block_size).astype(jnp.int32)
        col_piece = lax.dynamic_slice_in_dim(vectors, col_start, block_size, 1)
        row_piece = lax.dynamic_slice_in_dim(vectors, row_start, block_size, 1)
        direct = lax.dot_general(col_piece, block, (((1,), (1,)), ((), ())), preferred_element_type=jnp.float32)
        mirror = jnp.dot(row_piece, block, preferred_element_type=jnp.float32)
        direct = jnp.where(alive, direct, jnp.zeros_like(direct))
        mirror = jnp.where(alive, mirror, jnp.zeros_like(mirror))
        result = add_at(result, direct, row_start)
        result = add_at(result, mirror, col_start)
        return result, None

    result = jnp.zeros((vectors.shape[0], vectors.shape[1]), jnp.float32)
    result, _ = lax.scan(apply_block, result, (flat_tiles, global_rows, global_cols, live))
    return result
```

```python
import jax
import jax.numpy as jnp
from jax import lax
from jax.experimental import pallas as pl
from jax.experimental.pallas import tpu as pltpu
from jax.sharding import PartitionSpec as P

NX, NH, NC = 4, 2, 2
NY, NZ = 4, 8
VECS, BLK, SLOTS = 16, 512, 8
LANES = 128
LT = BLK // LANES
EXPO = SLOTS * LT
INDEX = EXPO + 1
MSG = INDEX + 1
MESH = pl.DeviceIdType.MESH
TINY = 2.0 ** -110


def exponent_of(most):
    return jnp.ceil(jnp.log2(jnp.maximum(most, TINY)) - 14.98)


def coded(values, inverse):
    return jnp.round(values * inverse).astype(jnp.int32).astype(jnp.int16)


def decoded(code):
    return code.astype(jnp.int32).astype(jnp.float32)


def most_of(parts):
    most = jnp.abs(parts[0])
    for part in parts[1:]:
        most = jnp.maximum(most, jnp.abs(part))
    return most


def kernel(
    vec, tiles, br, bc, cnt, out,
    rowbuf, colbuf, tilebuf, prod, ymsg, cmsg, dec, idxb, acc,
    zsend, zrecv, xsend, xrecv, hsend, hrecv, own,
    tsem, ys, yr, zs, zr, cs, cr, ss, sr, ms, mr, ks, kr, ps, pr, xs, xr, hs, hr,
):
    me_r, me_c = lax.axis_index("row"), lax.axis_index("col")
    x, h, core = me_r // (NH * NC), (me_r // NC) % NH, me_r % NC
    y, z = me_c // NZ, me_c % NZ

    def row_of(xx, hh, cc):
        return (xx * NH + hh) * NC + cc

    def col_of(yy, zz):
        return yy * NZ + zz

    def y_at(d):
        return (y + d + NY) % NY

    def z_at(d):
        return (z + d + NZ) % NZ

    def x_at(d):
        return (x + d + NX) % NX

    sibling = (row_of(x, h, 1 - core), me_c)
    far = (row_of(x, 1 - h, core), me_c)
    x_peer = [None] + [(row_of(x_at(d), h, core), me_c) for d in range(1, NX)]
    y_peer = [None] + [(me_r, col_of(y_at(d), z)) for d in range(1, NY)]
    z_peer = [None] + [(me_r, col_of(y, z_at(d))) for d in range(1, NZ)]

    def remote(src, dst, send, recv, device):
        return pltpu.make_async_remote_copy(
            src_ref=src, dst_ref=dst, send_sem=send, recv_sem=recv,
            device_id=device, device_id_type=MESH,
        )

    sent = []

    def send(*args):
        copy = remote(*args)
        copy.start()
        sent.append(copy)

    for s in range(SLOTS):
        pltpu.make_async_copy(tiles.at[s], tilebuf.at[s], tsem.at[s]).start()
    for k in range(2):
        piece = vec[:, k * BLK:(k + 1) * BLK]
        rowbuf[2 * me_c + k] = piece
        colbuf[2 * me_r + k] = piece

    barrier = pltpu.get_barrier_semaphore()
    partners = [sibling, far] + x_peer[1:] + y_peer[1:] + z_peer[1:]
    for device in partners:
        pl.semaphore_signal(barrier, inc=1, device_id=device, device_id_type=MESH)
    pl.semaphore_wait(barrier, len(partners))

    def row_chunk(dy, dz):
        return rowbuf.at[pl.ds(2 * col_of(y_at(-dy), z_at(-dz)), 2)]

    def col_chunk(d, e, cc):
        return colbuf.at[pl.ds(2 * row_of(x_at(-d), (h + e) % NH, cc), 2)]

    def relay(way, hop, i):
        chunk = row_chunk(i, way * hop)
        w = 0 if way > 0 else 1
        send(chunk, chunk, zs.at[w, hop, i], zr.at[w, hop, i], z_peer[way % NZ])

    def relay_wait(way, hop, i):
        chunk = row_chunk(i, way * (hop + 1))
        w = 0 if way > 0 else 1
        remote(chunk, chunk, zs.at[w, hop, i], zr.at[w, hop, i], z_peer[1]).wait_recv()

    def last_goes(way, i):
        return (i < NY // 2) == (way > 0)

    mine_row, mine_col = row_chunk(0, 0), col_chunk(0, 0, core)
    relay(1, 0, 0)
    relay(-1, 0, 0)
    send(mine_col, mine_col, cs.at[0, 1], cr.at[0, 1], far)
    for d in range(1, NY):
        send(mine_row, mine_row, ys.at[d], yr.at[d], y_peer[d])
    for d in range(1, NX):
        send(mine_col, mine_col, cs.at[d, 0], cr.at[d, 0], x_peer[d])
    send(mine_col, mine_col, ss.at[0, 0], sr.at[0, 0], sibling)

    for i in range(1, NY):
        chunk = row_chunk(i, 0)
        remote(chunk, chunk, ys.at[i], yr.at[i], y_peer[1]).wait_recv()
        relay(1, 0, i)
        relay(-1, 0, i)

    def col_wait(d, e):
        chunk = col_chunk(d, e, core)
        remote(chunk, chunk, cs.at[d, e], cr.at[d, e], far).wait_recv()

    col_wait(0, 1)
    theirs = col_chunk(0, 1, core)
    for d in range(1, NX):
        send(theirs, theirs, cs.at[d, 1], cr.at[d, 1], x_peer[d])
    send(theirs, theirs, ss.at[0, 1], sr.at[0, 1], sibling)

    for i in range(NY):
        for way in (1, -1):
            relay_wait(way, 0, i)
            relay(way, 1, i)

    for e in range(NH):
        for d in range(1, NX):
            col_wait(d, e)
            chunk = col_chunk(d, e, core)
            send(chunk, chunk, ss.at[d, e], sr.at[d, e], sibling)

    for i in range(NY):
        for way in (1, -1):
            relay_wait(way, 1, i)
            relay(way, 2, i)

    for e in range(NH):
        for d in range(NX):
            chunk = col_chunk(d, e, 1 - core)
            remote(chunk, chunk, ss.at[d, e], sr.at[d, e], sibling).wait_recv()

    live = cnt[0]
    lane_row = lax.broadcasted_iota(jnp.int32, (VECS, LANES), 0)

    def lane_parts(value):
        return [value[:, j * LANES:(j + 1) * LANES] for j in range(LT)]

    def products(pieces, where, to, contract, wait, msg):
        def one(s, most):
            if wait:
                pltpu.make_async_copy(tiles.at[s], tilebuf.at[s], tsem.at[s]).wait()
            value = lax.dot_general(
                pieces[where[s]], tilebuf[s], (((1,), (contract,)), ((), ())),
                preferred_element_type=jnp.float32,
            )
            value = jnp.where(s < live, value, 0.0)
            prod[s] = value
            return jnp.maximum(most, most_of(lane_parts(value)))

        most = lax.fori_loop(0, SLOTS, one, jnp.zeros((VECS, LANES), jnp.float32))
        exponent = exponent_of(most)
        inverse = 1.0 / jnp.exp2(exponent)

        def code(s, carry):
            for j, part in enumerate(lane_parts(prod[s])):
                msg[0, s * LT + j] = coded(part, inverse)
            return carry

        lax.fori_loop(0, SLOTS, code, 0)
        msg[0, EXPO] = exponent.astype(jnp.int32).astype(jnp.int16)
        index = jnp.full((VECS, LANES), -1, jnp.int32)
        for s in range(SLOTS):
            index = jnp.where(lane_row == s, jnp.where(s < live, to[s], -1), index)
        msg[0, INDEX] = index.astype(jnp.int16)

    def combine(msg, sources, target_of):
        for n in range(sources):
            scale = jnp.exp2(decoded(msg[n, EXPO]))
            index = msg[n, INDEX].astype(jnp.int32)
            for s in range(SLOTS):
                idxb[n * SLOTS + s] = jnp.broadcast_to(index[s:s + 1], (VECS, LANES))

            def open_slot(t, carry):
                dec[n * SLOTS * LT + t] = decoded(msg[n, t]) * scale
                return carry

            lax.fori_loop(0, SLOTS * LT, open_slot, 0)

        def lane_tile(j, carry):
            def candidate(c, sums):
                value, index = dec[c * LT + j], idxb[c]
                return tuple(
                    total + jnp.where(index == target_of(t), value, 0.0)
                    for t, total in enumerate(sums)
                )

            zero = jnp.zeros((VECS, LANES), jnp.float32)
            sums = lax.fori_loop(0, sources * SLOTS, candidate, (zero,) * 16)
            for t in range(16):
                acc[t, j] = sums[t]
            return carry

        lax.fori_loop(0, LT, lane_tile, 0)

    products(colbuf, bc, br, 1, True, ymsg)
    for d in range(1, NY):
        send(ymsg.at[0], ymsg.at[d], ps.at[d], pr.at[d], y_peer[d])

    for i in range(NY):
        for way in (1, -1):
            relay_wait(way, 2, i)
            if last_goes(way, i):
                relay(way, 3, i)
    for i in range(NY):
        relay_wait(1 if last_goes(1, i) else -1, 3, i)

    products(rowbuf, br, bc, 0, False, cmsg)
    send(cmsg.at[0], cmsg.at[1], ms.at[0], mr.at[0], sibling)

    for d in range(1, NY):
        remote(ymsg.at[0], ymsg.at[d], ps.at[d], pr.at[d], y_peer[1]).wait_recv()
    combine(ymsg, NY, lambda t: 2 * col_of(y, 0) + t)

    def code_chunk(parts, dst, first):
        exponent = exponent_of(most_of(parts))
        inverse = 1.0 / jnp.exp2(exponent)
        for t, part in enumerate(parts):
            dst[first + t] = coded(part, inverse)
        dst[first + len(parts)] = exponent.astype(jnp.int32).astype(jnp.int16)

    for d in range(1, NZ):
        to = z_at(d)
        code_chunk([acc[2 * to + k, j] for k in range(2) for j in range(LT)], zsend.at[d], 0)
        send(zsend.at[d], zrecv.at[d], ks.at[d], kr.at[d], z_peer[d])
    for k in range(2):
        for j in range(LT):
            own[k * LT + j] = acc[2 * z + k, j]

    remote(cmsg.at[0], cmsg.at[1], ms.at[0], mr.at[0], sibling).wait_recv()
    combine(cmsg, NC, lambda t: (t // 2) * 2 * NC + 2 * core + t % 2)
    CH = 2 * LT + 1
    for d in range(1, NX):
        for e in range(NH):
            chip = x_at(d) * NH + (h + e) % NH
            code_chunk([acc[2 * chip + k, j] for k in range(2) for j in range(LT)], xsend.at[d], e * CH)
        send(xsend.at[d], xrecv.at[d], xs.at[d], xr.at[d], x_peer[d])
    for d in range(1, NX):
        remote(xsend.at[d], xrecv.at[d], xs.at[d], xr.at[d], x_peer[1]).wait_recv()

    def opened(msg, first):
        scale = jnp.exp2(decoded(msg[first + 2 * LT]))
        return [decoded(msg[first + t]) * scale for t in range(2 * LT)]

    def with_x(e):
        chip = x * NH + (h + e) % NH
        parts = [acc[2 * chip + k, j] for k in range(2) for j in range(LT)]
        for d in range(1, NX):
            parts = [a + b for a, b in zip(parts, opened(xrecv.at[d], e * CH))]
        return parts

    code_chunk(with_x(1), hsend, 0)
    send(hsend, hrecv, hs.at[0], hr.at[0], far)
    total = [a + own[t] for t, a in enumerate(with_x(0))]
    for d in range(1, NZ):
        remote(zsend.at[d], zrecv.at[d], ks.at[d], kr.at[d], z_peer[1]).wait_recv()
        total = [a + b for a, b in zip(total, opened(zrecv.at[d], 0))]
    remote(hsend, hrecv, hs.at[0], hr.at[0], far).wait_recv()
    total = [a + b for a, b in zip(total, opened(hrecv, 0))]
    for t, part in enumerate(total):
        out[:, t * LANES:(t + 1) * LANES] = part

    for copy in sent:
        copy.wait_send()


def on_device(vectors, tiles, block_rows, block_cols, counts):
    i16, f32, bf16 = jnp.int16, jnp.float32, jnp.bfloat16
    chunk = 2 * LT + 1
    dma = pltpu.SemaphoreType.DMA
    scratch = [
        pltpu.VMEM((2 * NY * NZ, VECS, BLK), bf16),
        pltpu.VMEM((2 * NX * NH * NC, VECS, BLK), bf16),
        pltpu.VMEM((SLOTS, BLK, BLK), bf16),
        pltpu.VMEM((SLOTS, VECS, BLK), f32),
        pltpu.VMEM((NY, MSG, VECS, LANES), i16),
        pltpu.VMEM((NC, MSG, VECS, LANES), i16),
        pltpu.VMEM((NY * SLOTS * LT, VECS, LANES), f32),
        pltpu.VMEM((NY * SLOTS, VECS, LANES), jnp.int32),
        pltpu.VMEM((16, LT, VECS, LANES), f32),
        pltpu.VMEM((NZ, chunk, VECS, LANES), i16),
        pltpu.VMEM((NZ, chunk, VECS, LANES), i16),
        pltpu.VMEM((NX, NH * chunk, VECS, LANES), i16),
        pltpu.VMEM((NX, NH * chunk, VECS, LANES), i16),
        pltpu.VMEM((chunk, VECS, LANES), i16),
        pltpu.VMEM((chunk, VECS, LANES), i16),
        pltpu.VMEM((2 * LT, VECS, LANES), f32),
        dma((SLOTS,)),
        dma((NY,)), dma((NY,)),
        dma((2, NZ // 2, NY)), dma((2, NZ // 2, NY)),
        dma((NX, NH)), dma((NX, NH)),
        dma((NX, NH)), dma((NX, NH)),
        dma((1,)), dma((1,)),
        dma((NZ,)), dma((NZ,)),
        dma((NY,)), dma((NY,)),
        dma((NX,)), dma((NX,)),
        dma((1,)), dma((1,)),
    ]
    return pl.pallas_call(
        kernel,
        out_shape=jax.ShapeDtypeStruct((VECS, 2 * BLK), f32),
        in_specs=[
            pl.BlockSpec(memory_space=pltpu.VMEM),
            pl.BlockSpec(memory_space=pl.ANY),
            pl.BlockSpec(memory_space=pltpu.SMEM),
            pl.BlockSpec(memory_space=pltpu.SMEM),
            pl.BlockSpec(memory_space=pltpu.SMEM),
        ],
        out_specs=pl.BlockSpec(memory_space=pltpu.VMEM),
        scratch_shapes=scratch,
        compiler_params=pltpu.CompilerParams(
            collective_id=0, has_side_effects=True, vmem_limit_bytes=40 * 2 ** 20
        ),
    )(
        vectors,
        tiles.reshape(SLOTS, BLK, BLK),
        block_rows.reshape(SLOTS),
        block_cols.reshape(SLOTS),
        counts.reshape(1),
    )


def solution(mesh):
    placed = (
        P(None, ("row", "col")),
        P("row", "col", None, None, None),
        P("row", "col", None),
        P("row", "col", None),
        P("row", "col"),
    )
    return jax.shard_map(
        on_device, mesh=mesh, in_specs=placed, out_specs=P(None, ("row", "col")), check_vma=False
    )
```

```python
import jax
import jax.numpy as jnp
from jax import lax
from jax.experimental import pallas as pl
from jax.experimental.pallas import tpu as pltpu
from jax.sharding import PartitionSpec as P

NX, NH, NC = 4, 2, 2
NY, NZ = 4, 8
VECS, BLK, SLOTS = 16, 512, 8
LANES = 128
LT = BLK // LANES
EXPO = SLOTS * LT
MSG = EXPO + 1
MESH = pl.DeviceIdType.MESH
TINY = 2.0 ** -110


def exponent_of(most):
    return jnp.ceil(jnp.log2(jnp.maximum(most, TINY)) - 14.98)


def coded(values, inverse):
    return jnp.round(values * inverse).astype(jnp.int32).astype(jnp.int16)


def decoded(code):
    return code.astype(jnp.int32).astype(jnp.float32)


def most_of(parts):
    most = jnp.abs(parts[0])
    for part in parts[1:]:
        most = jnp.maximum(most, jnp.abs(part))
    return most


def kernel(
    vec, tiles, br_hbm, bc_hbm, cnt_hbm, out,
    br, bc, cnt, rto, cto, rprev, rlast, cprev, clast,
    rowbuf, colbuf, tilebuf, prod, ymsg, cmsg, run,
    zsend, zrecv, xsend, xrecv, hsend, hrecv, own,
    isem, vsem, tsem, ys, yr, zs, zr, cs, cr, ss, sr, ms, mr, ks, kr, ps, pr, xs, xr, hs, hr, js, jr,
):
    me_r, me_c = lax.axis_index("row"), lax.axis_index("col")
    x, h, core = me_r // (NH * NC), (me_r // NC) % NH, me_r % NC
    y, z = me_c // NZ, me_c % NZ

    def row_of(xx, hh, cc):
        return (xx * NH + hh) * NC + cc

    def col_of(yy, zz):
        return yy * NZ + zz

    def y_at(d):
        return (y + d + NY) % NY

    def z_at(d):
        return (z + d + NZ) % NZ

    def x_at(d):
        return (x + d + NX) % NX

    sibling = (row_of(x, h, 1 - core), me_c)
    far = (row_of(x, 1 - h, core), me_c)
    x_peer = [None] + [(row_of(x_at(d), h, core), me_c) for d in range(1, NX)]
    y_peer = [None] + [(me_r, col_of(y_at(d), z)) for d in range(1, NY)]
    z_peer = [None] + [(me_r, col_of(y, z_at(d))) for d in range(1, NZ)]

    def remote(src, dst, send, recv, device):
        return pltpu.make_async_remote_copy(
            src_ref=src, dst_ref=dst, send_sem=send, recv_sem=recv,
            device_id=device, device_id_type=MESH,
        )

    sent = []

    def send(*args):
        copy = remote(*args)
        copy.start()
        sent.append(copy)

    barrier = pltpu.get_barrier_semaphore()
    partners = [sibling, far] + x_peer[1:] + y_peer[1:] + z_peer[1:]
    for device in partners:
        pl.semaphore_signal(barrier, inc=1, device_id=device, device_id_type=MESH)

    into = []
    for k in range(2):
        piece = vec.at[:, pl.ds(k * BLK, BLK)]
        into.append(pltpu.make_async_copy(piece, rowbuf.at[2 * me_c + k], vsem.at[k]))
        into.append(pltpu.make_async_copy(piece, colbuf.at[2 * me_r + k], vsem.at[2 + k]))
    into.append(pltpu.make_async_copy(br_hbm.at[0, 0], br, isem.at[0]))
    into.append(pltpu.make_async_copy(bc_hbm.at[0, 0], bc, isem.at[1]))
    into.append(pltpu.make_async_copy(cnt_hbm.at[0], cnt, isem.at[2]))
    for copy in into:
        copy.start()
    for s in range(SLOTS):
        pltpu.make_async_copy(tiles.at[0, 0, s], tilebuf.at[s], tsem.at[s]).start()
    for copy in into:
        copy.wait()
    live = cnt[0]
    for s in range(SLOTS):
        rto[0, s] = jnp.where(s < live, br[s], -1)
        cto[0, s] = jnp.where(s < live, bc[s], -1)
    pl.semaphore_wait(barrier, len(partners))

    def row_chunk(dy, dz):
        return rowbuf.at[pl.ds(2 * col_of(y_at(-dy), z_at(-dz)), 2)]

    def col_chunk(d, e, cc):
        return colbuf.at[pl.ds(2 * row_of(x_at(-d), (h + e) % NH, cc), 2)]

    def relay(way, hop, i):
        chunk = row_chunk(i, way * hop)
        w = 0 if way > 0 else 1
        send(chunk, chunk, zs.at[w, hop, i], zr.at[w, hop, i], z_peer[way % NZ])

    def relay_wait(way, hop, i):
        chunk = row_chunk(i, way * (hop + 1))
        w = 0 if way > 0 else 1
        remote(chunk, chunk, zs.at[w, hop, i], zr.at[w, hop, i], z_peer[1]).wait_recv()

    def last_goes(way, i):
        return (i < NY // 2) == (way > 0)

    def col_wait(d, e):
        chunk = col_chunk(d, e, core)
        remote(chunk, chunk, cs.at[d, e], cr.at[d, e], far).wait_recv()

    def to_sibling(d, e):
        chunk = col_chunk(d, e, core)
        send(chunk, chunk, ss.at[d, e], sr.at[d, e], sibling)

    def tables(to, prev, last, sources, target_of):
        names = [to[n, s] for n in range(sources) for s in range(SLOTS)]
        for c, name in enumerate(names):
            found = jnp.int32(len(names))
            for earlier in range(c):
                found = jnp.where(names[earlier] == name, earlier, found)
            prev[c] = found
        for t in range(16):
            found = jnp.int32(len(names))
            for c, name in enumerate(names):
                found = jnp.where(name == target_of(t), c, found)
            last[t] = found

    mine_row, mine_col = row_chunk(0, 0), col_chunk(0, 0, core)
    send(mine_col, mine_col, cs.at[0, 1], cr.at[0, 1], far)
    for d in range(1, NY):
        send(mine_row, mine_row, ys.at[d], yr.at[d], y_peer[d])
    relay(1, 0, 0)
    relay(-1, 0, 0)
    for d in range(1, NX):
        send(mine_col, mine_col, cs.at[d, 0], cr.at[d, 0], x_peer[d])
    to_sibling(0, 0)
    send(cto.at[0], cto.at[1], js.at[0], jr.at[0], sibling)
    for d in range(1, NY):
        send(rto.at[0], rto.at[d], js.at[d], jr.at[d], y_peer[d])

    remote(cto.at[0], cto.at[1], js.at[0], jr.at[0], sibling).wait_recv()
    tables(cto, cprev, clast, NC, lambda t: (t // 2) * 2 * NC + 2 * core + t % 2)

    for i in range(1, NY):
        chunk = row_chunk(i, 0)
        remote(chunk, chunk, ys.at[i], yr.at[i], y_peer[1]).wait_recv()
        relay(1, 0, i)
        relay(-1, 0, i)
    for way in (1, -1):
        relay_wait(way, 0, 0)
        relay(way, 1, 0)

    for d in range(1, NY):
        remote(rto.at[0], rto.at[d], js.at[d], jr.at[d], y_peer[1]).wait_recv()
    tables(rto, rprev, rlast, NY, lambda t: 2 * col_of(y, 0) + t)

    col_wait(0, 1)
    theirs = col_chunk(0, 1, core)
    for d in range(1, NX):
        send(theirs, theirs, cs.at[d, 1], cr.at[d, 1], x_peer[d])
    to_sibling(0, 1)
    for d in range(1, NX):
        col_wait(d, 0)
        to_sibling(d, 0)

    for i in range(1, NY):
        for way in (1, -1):
            relay_wait(way, 0, i)
            relay(way, 1, i)
    for way in (1, -1):
        relay_wait(way, 1, 0)
        relay(way, 2, 0)

    for d in range(1, NX):
        col_wait(d, 1)
        to_sibling(d, 1)

    for i in range(1, NY):
        for way in (1, -1):
            relay_wait(way, 1, i)
            relay(way, 2, i)

    for e in range(NH):
        for d in range(NX):
            chunk = col_chunk(d, e, 1 - core)
            remote(chunk, chunk, ss.at[d, e], sr.at[d, e], sibling).wait_recv()

    def lane_parts(value):
        return [value[:, j * LANES:(j + 1) * LANES] for j in range(LT)]

    def products(pieces, where, contract, wait, msg):
        most = jnp.zeros((VECS, LANES), jnp.float32)
        for s in range(SLOTS):
            if wait:
                pltpu.make_async_copy(tiles.at[0, 0, s], tilebuf.at[s], tsem.at[s]).wait()
            value = lax.dot_general(
                pieces[where[s]], tilebuf[s], (((1,), (contract,)), ((), ())),
                preferred_element_type=jnp.float32,
            )
            value = jnp.where(s < live, value, 0.0)
            prod[s] = value
            most = jnp.maximum(most, most_of(lane_parts(value)))
        exponent = exponent_of(most)
        inverse = 1.0 / jnp.exp2(exponent)
        for s in range(SLOTS):
            for j, part in enumerate(lane_parts(prod[s])):
                msg[0, s * LT + j] = coded(part, inverse)
        msg[0, EXPO] = exponent.astype(jnp.int32).astype(jnp.int16)

    def combine(msg, sources, prev):
        run[sources * SLOTS] = jnp.zeros((LT, VECS, LANES), jnp.float32)
        for n in range(sources):
            scale = jnp.exp2(decoded(msg[n, EXPO]))

            def slot(s, carry):
                c = n * SLOTS + s
                before = run[prev[c]]
                for j in range(LT):
                    run[c, j] = decoded(msg[n, s * LT + j]) * scale + before[j]
                return carry

            lax.fori_loop(0, SLOTS, slot, 0)

    def block_parts(last, t):
        value = run[last[t]]
        return [value[j] for j in range(LT)]

    products(colbuf, bc, 1, True, ymsg)
    for d in range(1, NY):
        send(ymsg.at[0], ymsg.at[d], ps.at[d], pr.at[d], y_peer[d])

    for i in range(NY):
        for way in (1, -1):
            relay_wait(way, 2, i)
            if last_goes(way, i):
                relay(way, 3, i)
    for i in range(NY):
        relay_wait(1 if last_goes(1, i) else -1, 3, i)

    products(rowbuf, br, 0, False, cmsg)
    send(cmsg.at[0], cmsg.at[1], ms.at[0], mr.at[0], sibling)

    def code_chunk(parts, dst, first):
        exponent = exponent_of(most_of(parts))
        inverse = 1.0 / jnp.exp2(exponent)
        for t, part in enumerate(parts):
            dst[first + t] = coded(part, inverse)
        dst[first + len(parts)] = exponent.astype(jnp.int32).astype(jnp.int16)

    def chip_parts(xx, e):
        chip = xx * NH + (h + e) % NH
        return block_parts(clast, 2 * chip) + block_parts(clast, 2 * chip + 1)

    remote(cmsg.at[0], cmsg.at[1], ms.at[0], mr.at[0], sibling).wait_recv()
    combine(cmsg, NC, cprev)
    CH = 2 * LT + 1
    for d in range(1, NX):
        for e in range(NH):
            code_chunk(chip_parts(x_at(d), e), xsend.at[d], e * CH)
        send(xsend.at[d], xrecv.at[d], xs.at[d], xr.at[d], x_peer[d])
    for e in range(NH):
        for t, part in enumerate(chip_parts(x, e)):
            own[e, t] = part

    for d in range(1, NY):
        remote(ymsg.at[0], ymsg.at[d], ps.at[d], pr.at[d], y_peer[1]).wait_recv()
    combine(ymsg, NY, rprev)
    for d in range(1, NZ):
        to = z_at(d)
        code_chunk(block_parts(rlast, 2 * to) + block_parts(rlast, 2 * to + 1), zsend.at[d], 0)
        send(zsend.at[d], zrecv.at[d], ks.at[d], kr.at[d], z_peer[d])

    def opened(msg, first):
        scale = jnp.exp2(decoded(msg[first + 2 * LT]))
        return [decoded(msg[first + t]) * scale for t in range(2 * LT)]

    for d in range(1, NX):
        remote(xsend.at[d], xrecv.at[d], xs.at[d], xr.at[d], x_peer[1]).wait_recv()

    def with_x(e):
        parts = [own[e, t] for t in range(2 * LT)]
        for d in range(1, NX):
            parts = [a + b for a, b in zip(parts, opened(xrecv.at[d], e * CH))]
        return parts

    code_chunk(with_x(1), hsend, 0)
    send(hsend, hrecv, hs.at[0], hr.at[0], far)
    mine = block_parts(rlast, 2 * z) + block_parts(rlast, 2 * z + 1)
    total = [a + b for a, b in zip(with_x(0), mine)]
    for d in range(1, NZ):
        remote(zsend.at[d], zrecv.at[d], ks.at[d], kr.at[d], z_peer[1]).wait_recv()
        total = [a + b for a, b in zip(total, opened(zrecv.at[d], 0))]
    remote(hsend, hrecv, hs.at[0], hr.at[0], far).wait_recv()
    total = [a + b for a, b in zip(total, opened(hrecv, 0))]
    for t, part in enumerate(total):
        out[:, t * LANES:(t + 1) * LANES] = part

    for copy in sent:
        copy.wait_send()


def on_device(vectors, tiles, block_rows, block_cols, counts):
    i16, f32, bf16 = jnp.int16, jnp.float32, jnp.bfloat16
    chunk = 2 * LT + 1
    dma = pltpu.SemaphoreType.DMA

    def smem(shape):
        return pltpu.SMEM(shape, jnp.int32)

    scratch = [
        smem((SLOTS,)), smem((SLOTS,)), smem((1,)),
        smem((NY, SLOTS)), smem((NC, SLOTS)),
        smem((NY * SLOTS,)), smem((16,)),
        smem((NC * SLOTS,)), smem((16,)),
        pltpu.VMEM((2 * NY * NZ, VECS, BLK), bf16),
        pltpu.VMEM((2 * NX * NH * NC, VECS, BLK), bf16),
        pltpu.VMEM((SLOTS, BLK, BLK), bf16),
        pltpu.VMEM((SLOTS, VECS, BLK), f32),
        pltpu.VMEM((NY, MSG, VECS, LANES), i16),
        pltpu.VMEM((NC, MSG, VECS, LANES), i16),
        pltpu.VMEM((NY * SLOTS + 1, LT, VECS, LANES), f32),
        pltpu.VMEM((NZ, chunk, VECS, LANES), i16),
        pltpu.VMEM((NZ, chunk, VECS, LANES), i16),
        pltpu.VMEM((NX, NH * chunk, VECS, LANES), i16),
        pltpu.VMEM((NX, NH * chunk, VECS, LANES), i16),
        pltpu.VMEM((chunk, VECS, LANES), i16),
        pltpu.VMEM((chunk, VECS, LANES), i16),
        pltpu.VMEM((NH, 2 * LT, VECS, LANES), f32),
        dma((3,)), dma((4,)),
        dma((SLOTS,)),
        dma((NY,)), dma((NY,)),
        dma((2, NZ // 2, NY)), dma((2, NZ // 2, NY)),
        dma((NX, NH)), dma((NX, NH)),
        dma((NX, NH)), dma((NX, NH)),
        dma((1,)), dma((1,)),
        dma((NZ,)), dma((NZ,)),
        dma((NY,)), dma((NY,)),
        dma((NX,)), dma((NX,)),
        dma((1,)), dma((1,)),
        dma((NY,)), dma((NY,)),
    ]
    return pl.pallas_call(
        kernel,
        out_shape=jax.ShapeDtypeStruct((VECS, 2 * BLK), f32),
        in_specs=[pl.BlockSpec(memory_space=pltpu.HBM)] * 5,
        out_specs=pl.BlockSpec(memory_space=pltpu.VMEM),
        scratch_shapes=scratch,
        compiler_params=pltpu.CompilerParams(
            collective_id=0, has_side_effects=True, vmem_limit_bytes=64 * 2 ** 20
        ),
    )(vectors, tiles, block_rows, block_cols, counts)


def solution(mesh):
    placed = (
        P(None, ("row", "col")),
        P("row", "col", None, None, None),
        P("row", "col", None),
        P("row", "col", None),
        P("row", "col"),
    )
    return jax.shard_map(
        on_device, mesh=mesh, in_specs=placed, out_specs=P(None, ("row", "col")), check_vma=False
    )
```

```python
import jax
import jax.numpy as jnp
from jax import lax
from jax.experimental import pallas as pl
from jax.experimental.pallas import tpu as pltpu
from jax.sharding import PartitionSpec as P

NX, NH, NC = 4, 2, 2
NY, NZ = 4, 8
VECS, BLK, SLOTS = 16, 512, 8
SQ, PLACES = NY, NZ
WAYS = (1, -1)
LANES = 128
LT = BLK // LANES
HALF = SLOTS // 2
PART = HALF * LT + 1
MESH = pl.DeviceIdType.MESH
TINY = 2.0 ** -110


def exponent_of(most):
    return jnp.ceil(jnp.log2(jnp.maximum(most, TINY)) - 14.98)


def coded(values, inverse):
    return jnp.round(values * inverse).astype(jnp.int32).astype(jnp.int16)


def decoded(code):
    return code.astype(jnp.int32).astype(jnp.float32)


def most_of(parts):
    most = jnp.abs(parts[0])
    for part in parts[1:]:
        most = jnp.maximum(most, jnp.abs(part))
    return most


def kernel(
    vec, tiles, br_hbm, bc_hbm, cnt_hbm, out,
    br, bc, cnt, rto, cto, rprev, rlast, cprev, clast,
    rowbuf, colbuf, tilebuf, turned, ymsg, cmsg, run,
    zsend, zrecv, xsend, xrecv, hsend, hrecv, own,
    isem, vsem, tsem, ys, yr, zs, zr, qs, qr, us, ur, cs, cr, ss, sr, ms, mr, ks, kr, ps, pr, xs, xr, hs, hr, js, jr,
):
    me_r, me_c = lax.axis_index("row"), lax.axis_index("col")
    x, h, core = me_r // (NH * NC), (me_r // NC) % NH, me_r % NC
    y, z = me_c // NZ, me_c % NZ

    def row_of(xx, hh, cc):
        return (xx * NH + hh) * NC + cc

    def col_of(yy, zz):
        return yy * NZ + zz

    def y_at(d):
        return (y + d + NY) % NY

    def z_at(d):
        return (z + d + NZ) % NZ

    def x_at(d):
        return (x + d + NX) % NX

    sibling = (row_of(x, h, 1 - core), me_c)
    far = (row_of(x, 1 - h, core), me_c)
    x_peer = [None] + [(row_of(x_at(d), h, core), me_c) for d in range(1, NX)]
    y_peer = [None] + [(me_r, col_of(y_at(d), z)) for d in range(1, NY)]
    z_peer = [None] + [(me_r, col_of(y, z_at(d))) for d in range(1, NZ)]

    def remote(src, dst, send, recv, device):
        return pltpu.make_async_remote_copy(
            src_ref=src, dst_ref=dst, send_sem=send, recv_sem=recv,
            device_id=device, device_id_type=MESH,
        )

    sent = []

    def send(*args):
        copy = remote(*args)
        copy.start()
        sent.append(copy)

    barrier = pltpu.get_barrier_semaphore()
    partners = [sibling, far] + x_peer[1:] + y_peer[1:] + z_peer[1:]
    for device in partners:
        pl.semaphore_signal(barrier, inc=1, device_id=device, device_id_type=MESH)

    local = [
        pltpu.make_async_copy(br_hbm.at[0, 0], br, isem.at[0]),
        pltpu.make_async_copy(bc_hbm.at[0, 0], bc, isem.at[1]),
        pltpu.make_async_copy(cnt_hbm.at[0], cnt, isem.at[2]),
        pltpu.make_async_copy(vec, rowbuf.at[me_c], vsem.at[0]),
        pltpu.make_async_copy(vec, colbuf.at[me_r], vsem.at[1]),
    ]
    for copy in local:
        copy.start()
    pl.semaphore_wait(barrier, len(partners))

    def row_chunk(dy, dz):
        return rowbuf.at[col_of(y_at(-dy), z_at(-dz))]

    def col_chunk(d, e, cc):
        return colbuf.at[row_of(x_at(-d), (h + e) % NH, cc)]

    def pass_on(way, hop, i):
        chunk = row_chunk(i, way * hop)
        source = vec if hop == 0 and i == 0 else chunk
        w = WAYS.index(way)
        send(source, chunk, qs.at[w, hop, i], qr.at[w, hop, i], z_peer[way % NZ])

    def passed(way, hop, i):
        chunk = row_chunk(i, way * (hop + 1))
        w = WAYS.index(way)
        remote(chunk, chunk, qs.at[w, hop, i], qr.at[w, hop, i], z_peer[1]).wait_recv()

    def step(hop, group):
        for i in group:
            for way in WAYS:
                passed(way, hop, i)
                pass_on(way, hop + 1, i)

    def col_wait(d, e):
        chunk = col_chunk(d, e, core)
        remote(chunk, chunk, cs.at[d, e], cr.at[d, e], far).wait_recv()

    def to_sibling(d, e):
        chunk = col_chunk(d, e, core)
        source = vec if d == 0 and e == 0 else chunk
        send(source, chunk, ss.at[d, e], sr.at[d, e], sibling)

    def tables(to, prev, last, sources, target_of):
        names = [to[n, s] for n in range(sources) for s in range(SLOTS)]
        for c, name in enumerate(names):
            found = jnp.int32(len(names))
            for earlier in range(c):
                found = jnp.where(names[earlier] == name, earlier, found)
            prev[c] = found
        for t in range(16):
            found = jnp.int32(len(names))
            for c, name in enumerate(names):
                found = jnp.where(name == target_of(t), c, found)
            last[t] = found

    mine_row, mine_col = row_chunk(0, 0), col_chunk(0, 0, core)
    send(vec, mine_col, cs.at[0, 1], cr.at[0, 1], far)
    for d in range(1, NY):
        send(vec, mine_row, ys.at[d], yr.at[d], y_peer[d])
    for d in range(1, NX):
        send(vec, mine_col, cs.at[d, 0], cr.at[d, 0], x_peer[d])
    send(vec, mine_row, zs.at[0], zr.at[0], z_peer[NZ // 2])
    for way in WAYS:
        pass_on(way, 0, 0)
    to_sibling(0, 0)

    for s in range(SLOTS):
        pltpu.make_async_copy(tiles.at[0, 0, s], tilebuf.at[s], tsem.at[s]).start()
    for copy in local:
        copy.wait()
    live = cnt[0]
    for s in range(SLOTS):
        rto[0, s] = jnp.where(s < live, br[s], -1)
        cto[0, s] = jnp.where(s < live, bc[s], -1)
    send(cto.at[0], cto.at[1], js.at[0], jr.at[0], sibling)
    for d in range(1, SQ):
        send(rto.at[0], rto.at[d], js.at[d], jr.at[d], y_peer[d])

    for s in range(SLOTS):
        pltpu.make_async_copy(tiles.at[0, 0, s], tilebuf.at[s], tsem.at[s]).wait()

    def turn(s, carry):
        turned[s] = tilebuf[s].T
        return carry

    lax.fori_loop(0, SLOTS, turn, 0)

    for i in range(1, NY):
        chunk = row_chunk(i, 0)
        remote(chunk, chunk, ys.at[i], yr.at[i], y_peer[1]).wait_recv()
        for way in WAYS:
            pass_on(way, 0, i)
    step(0, [0])

    col_wait(0, 1)
    theirs = col_chunk(0, 1, core)
    for d in range(1, NX):
        send(theirs, theirs, cs.at[d, 1], cr.at[d, 1], x_peer[d])
    to_sibling(0, 1)

    chunk = row_chunk(0, NZ // 2)
    remote(chunk, chunk, zs.at[0], zr.at[0], z_peer[1]).wait_recv()
    for d in range(1, NY):
        send(chunk, chunk, us.at[d], ur.at[d], y_peer[d])

    for d in range(1, NX):
        col_wait(d, 0)
        to_sibling(d, 0)
    step(0, range(1, NY))
    step(1, [0])
    for d in range(1, NX):
        col_wait(d, 1)
        to_sibling(d, 1)
    for e in range(NH):
        for d in range(NX):
            chunk = col_chunk(d, e, 1 - core)
            remote(chunk, chunk, ss.at[d, e], sr.at[d, e], sibling).wait_recv()

    def lane_parts(value):
        return [value[:, j * LANES:(j + 1) * LANES] for j in range(LT)]

    def products(pieces, where, blocks, msg, part):
        values = []
        for s in range(part * HALF, (part + 1) * HALF):
            pair = pieces[where[s] // 2]
            piece = jnp.where(where[s] % 2 == 0, pair[:, :BLK], pair[:, BLK:])
            value = jnp.dot(piece, blocks[s], preferred_element_type=jnp.float32)
            values += lane_parts(jnp.where(s < live, value, 0.0))
        exponent = exponent_of(most_of(values))
        inverse = 1.0 / jnp.exp2(exponent)
        for t, value in enumerate(values):
            msg[0, part, t] = coded(value, inverse)
        msg[0, part, PART - 1] = exponent.astype(jnp.int32).astype(jnp.int16)

    def combine(msg, sources, prev):
        run[sources * SLOTS] = jnp.zeros((LT, VECS, LANES), jnp.float32)
        for n in range(sources):
            for part in range(2):
                scale = jnp.exp2(decoded(msg[n, part, PART - 1]))

                def slot(s, carry):
                    c = n * SLOTS + part * HALF + s
                    before = run[prev[c]]
                    for j in range(LT):
                        run[c, j] = decoded(msg[n, part, s * LT + j]) * scale + before[j]
                    return carry

                lax.fori_loop(0, HALF, slot, 0)

    def block_parts(last, t):
        value = run[last[t]]
        return [value[j] for j in range(LT)]

    for part in range(2):
        products(colbuf, bc, turned, ymsg, part)
        for d in range(1, SQ):
            send(ymsg.at[0, part], ymsg.at[d, part], ps.at[d, part], pr.at[d, part], y_peer[d])

    step(1, range(1, NY))
    remote(cto.at[0], cto.at[1], js.at[0], jr.at[0], sibling).wait_recv()
    tables(cto, cprev, clast, NC, lambda t: (t // 2) * 2 * NC + 2 * core + t % 2)
    for d in range(1, SQ):
        remote(rto.at[0], rto.at[d], js.at[d], jr.at[d], y_peer[1]).wait_recv()
    tables(
        rto, rprev, rlast, SQ,
        lambda t: 2 * col_of(y, 0) + t,
    )

    for i in range(1, NY):
        chunk = row_chunk(i, NZ // 2)
        remote(chunk, chunk, us.at[i], ur.at[i], y_peer[1]).wait_recv()
    for i in range(NY):
        for way in WAYS:
            passed(way, 2, i)

    for part in range(2):
        products(rowbuf, br, tilebuf, cmsg, part)
        send(cmsg.at[0, part], cmsg.at[1, part], ms.at[part], mr.at[part], sibling)

    def code_chunk(parts, dst, first):
        exponent = exponent_of(most_of(parts))
        inverse = 1.0 / jnp.exp2(exponent)
        for t, part in enumerate(parts):
            dst[first + t] = coded(part, inverse)
        dst[first + len(parts)] = exponent.astype(jnp.int32).astype(jnp.int16)

    def chip_parts(xx, e):
        chip = xx * NH + (h + e) % NH
        return block_parts(clast, 2 * chip) + block_parts(clast, 2 * chip + 1)

    for part in range(2):
        remote(cmsg.at[0, part], cmsg.at[1, part], ms.at[part], mr.at[part], sibling).wait_recv()
    combine(cmsg, NC, cprev)
    CH = 2 * LT + 1
    for d in range(1, NX):
        for e in range(NH):
            code_chunk(chip_parts(x_at(d), e), xsend.at[d], e * CH)
        send(xsend.at[d], xrecv.at[d], xs.at[d], xr.at[d], x_peer[d])
    for e in range(NH):
        for t, part in enumerate(chip_parts(x, e)):
            own[e, t] = part

    def place_parts(q):
        first = 2 * z_at(q)
        return block_parts(rlast, first) + block_parts(rlast, first + 1)

    for d in range(1, SQ):
        for part in range(2):
            remote(ymsg.at[0, part], ymsg.at[d, part], ps.at[d, part], pr.at[d, part], y_peer[1]).wait_recv()
    combine(ymsg, SQ, rprev)
    for q in range(1, PLACES):
        code_chunk(place_parts(q), zsend.at[q], 0)
        send(zsend.at[q], zrecv.at[q], ks.at[q], kr.at[q], z_peer[q])

    def opened(msg, first):
        scale = jnp.exp2(decoded(msg[first + 2 * LT]))
        return [decoded(msg[first + t]) * scale for t in range(2 * LT)]

    for d in range(1, NX):
        remote(xsend.at[d], xrecv.at[d], xs.at[d], xr.at[d], x_peer[1]).wait_recv()

    def with_x(e):
        parts = [own[e, t] for t in range(2 * LT)]
        for d in range(1, NX):
            parts = [a + b for a, b in zip(parts, opened(xrecv.at[d], e * CH))]
        return parts

    code_chunk(with_x(1), hsend, 0)
    send(hsend, hrecv, hs.at[0], hr.at[0], far)
    total = [a + b for a, b in zip(with_x(0), place_parts(0))]
    for q in range(1, PLACES):
        remote(zsend.at[q], zrecv.at[q], ks.at[q], kr.at[q], z_peer[1]).wait_recv()
        total = [a + b for a, b in zip(total, opened(zrecv.at[q], 0))]
    remote(hsend, hrecv, hs.at[0], hr.at[0], far).wait_recv()
    total = [a + b for a, b in zip(total, opened(hrecv, 0))]
    for t, part in enumerate(total):
        out[:, t * LANES:(t + 1) * LANES] = part

    for copy in sent:
        copy.wait_send()


def on_device(vectors, tiles, block_rows, block_cols, counts):
    i16, f32, bf16 = jnp.int16, jnp.float32, jnp.bfloat16
    chunk = 2 * LT + 1
    dma = pltpu.SemaphoreType.DMA

    def smem(shape):
        return pltpu.SMEM(shape, jnp.int32)

    scratch = [
        smem((SLOTS,)), smem((SLOTS,)), smem((1,)),
        smem((SQ, SLOTS)), smem((NC, SLOTS)),
        smem((SQ * SLOTS,)), smem((16,)),
        smem((NC * SLOTS,)), smem((16,)),
        pltpu.VMEM((NY * NZ, VECS, 2 * BLK), bf16),
        pltpu.VMEM((NX * NH * NC, VECS, 2 * BLK), bf16),
        pltpu.VMEM((SLOTS, BLK, BLK), bf16),
        pltpu.VMEM((SLOTS, BLK, BLK), bf16),
        pltpu.VMEM((SQ, 2, PART, VECS, LANES), i16),
        pltpu.VMEM((NC, 2, PART, VECS, LANES), i16),
        pltpu.VMEM((SQ * SLOTS + 1, LT, VECS, LANES), f32),
        pltpu.VMEM((PLACES, chunk, VECS, LANES), i16),
        pltpu.VMEM((PLACES, chunk, VECS, LANES), i16),
        pltpu.VMEM((NX, NH * chunk, VECS, LANES), i16),
        pltpu.VMEM((NX, NH * chunk, VECS, LANES), i16),
        pltpu.VMEM((chunk, VECS, LANES), i16),
        pltpu.VMEM((chunk, VECS, LANES), i16),
        pltpu.VMEM((NH, 2 * LT, VECS, LANES), f32),
        dma((3,)), dma((2,)),
        dma((SLOTS,)),
        dma((NY,)), dma((NY,)),
        dma((1,)), dma((1,)),
        dma((2, NZ // 2 - 1, NY)), dma((2, NZ // 2 - 1, NY)),
        dma((NY,)), dma((NY,)),
        dma((NX, NH)), dma((NX, NH)),
        dma((NX, NH)), dma((NX, NH)),
        dma((2,)), dma((2,)),
        dma((PLACES,)), dma((PLACES,)),
        dma((SQ, 2)), dma((SQ, 2)),
        dma((NX,)), dma((NX,)),
        dma((1,)), dma((1,)),
        dma((SQ,)), dma((SQ,)),
    ]
    return pl.pallas_call(
        kernel,
        out_shape=jax.ShapeDtypeStruct((VECS, 2 * BLK), f32),
        in_specs=[pl.BlockSpec(memory_space=pltpu.HBM)] * 5,
        out_specs=pl.BlockSpec(memory_space=pltpu.VMEM),
        scratch_shapes=scratch,
        compiler_params=pltpu.CompilerParams(
            collective_id=0, has_side_effects=True, vmem_limit_bytes=64 * 2 ** 20
        ),
    )(vectors, tiles, block_rows, block_cols, counts)


def solution(mesh):
    placed = (
        P(None, ("row", "col")),
        P("row", "col", None, None, None),
        P("row", "col", None),
        P("row", "col", None),
        P("row", "col"),
    )
    return jax.shard_map(
        on_device, mesh=mesh, in_specs=placed, out_specs=P(None, ("row", "col")), check_vma=False
    )
```

```python
import jax
import jax.numpy as jnp
from jax import lax
from jax.experimental import pallas as pl
from jax.experimental.pallas import tpu as pltpu
from jax.sharding import PartitionSpec as P

NX, NH, NC = 4, 2, 2
NY, NZ = 4, 8
VECS, BLK, SLOTS = 16, 512, 8
SQ, PLACES = NY, NZ
WAYS = (1, -1)
LANES = 128
LT = BLK // LANES
HALF = SLOTS // 2
PART = HALF * LT + 1
LONE = LT + 1
MESH = pl.DeviceIdType.MESH
TINY = 2.0 ** -110


def exponent_of(most):
    return jnp.ceil(jnp.log2(jnp.maximum(most, TINY)) - 14.98)


def coded(values, inverse):
    return jnp.round(values * inverse).astype(jnp.int32).astype(jnp.int16)


def decoded(code):
    return code.astype(jnp.int32).astype(jnp.float32)


def most_of(parts):
    most = jnp.abs(parts[0])
    for part in parts[1:]:
        most = jnp.maximum(most, jnp.abs(part))
    return most


def kernel(
    vec, tiles, br_hbm, bc_hbm, cnt_hbm, out,
    br, bc, cnt, rto, cto, rprev, rlast, cprev, clast,
    rowbuf, colbuf, tilebuf, turned, ymsg, cmsg, lone, lent, kept, run,
    zsend, zrecv, xsend, xrecv, hsend, hrecv, own,
    isem, vsem, tsem, ys, yr, zs, zr, qs, qr, us, ur, cs, cr, ss, sr, ms, mr, ks, kr, ps, pr, xs, xr, hs, hr, js, jr, es, er, fs, fr,
):
    me_r, me_c = lax.axis_index("row"), lax.axis_index("col")
    x, h, core = me_r // (NH * NC), (me_r // NC) % NH, me_r % NC
    y, z = me_c // NZ, me_c % NZ

    def row_of(xx, hh, cc):
        return (xx * NH + hh) * NC + cc

    def col_of(yy, zz):
        return yy * NZ + zz

    def y_at(d):
        return (y + d + NY) % NY

    def z_at(d):
        return (z + d + NZ) % NZ

    def x_at(d):
        return (x + d + NX) % NX

    sibling = (row_of(x, h, 1 - core), me_c)
    far = (row_of(x, 1 - h, core), me_c)
    x_peer = [None] + [(row_of(x_at(d), h, core), me_c) for d in range(1, NX)]
    y_peer = [None] + [(me_r, col_of(y_at(d), z)) for d in range(1, NY)]
    z_peer = [None] + [(me_r, col_of(y, z_at(d))) for d in range(1, NZ)]

    def remote(src, dst, send, recv, device):
        return pltpu.make_async_remote_copy(
            src_ref=src, dst_ref=dst, send_sem=send, recv_sem=recv,
            device_id=device, device_id_type=MESH,
        )

    sent = []

    def send(*args):
        copy = remote(*args)
        copy.start()
        sent.append(copy)

    barrier = pltpu.get_barrier_semaphore()
    partners = [sibling, far] + x_peer[1:] + y_peer[1:] + z_peer[1:]
    for device in partners:
        pl.semaphore_signal(barrier, inc=1, device_id=device, device_id_type=MESH)

    local = [
        pltpu.make_async_copy(br_hbm.at[0, 0], br, isem.at[0]),
        pltpu.make_async_copy(bc_hbm.at[0, 0], bc, isem.at[1]),
        pltpu.make_async_copy(cnt_hbm.at[0], cnt, isem.at[2]),
        pltpu.make_async_copy(vec, rowbuf.at[me_c], vsem.at[0]),
        pltpu.make_async_copy(vec, colbuf.at[me_r], vsem.at[1]),
    ]
    for copy in local:
        copy.start()
    pl.semaphore_wait(barrier, len(partners))

    def row_chunk(dy, dz):
        return rowbuf.at[col_of(y_at(-dy), z_at(-dz))]

    def col_chunk(d, e, cc):
        return colbuf.at[row_of(x_at(-d), (h + e) % NH, cc)]

    def pass_on(way, hop, i):
        chunk = row_chunk(i, way * hop)
        source = vec if hop == 0 and i == 0 else chunk
        w = WAYS.index(way)
        send(source, chunk, qs.at[w, hop, i], qr.at[w, hop, i], z_peer[way % NZ])

    def passed(way, hop, i):
        chunk = row_chunk(i, way * (hop + 1))
        w = WAYS.index(way)
        remote(chunk, chunk, qs.at[w, hop, i], qr.at[w, hop, i], z_peer[1]).wait_recv()

    def step(hop, group):
        for i in group:
            for way in WAYS:
                passed(way, hop, i)
                pass_on(way, hop + 1, i)

    def col_wait(d, e):
        chunk = col_chunk(d, e, core)
        remote(chunk, chunk, cs.at[d, e], cr.at[d, e], far).wait_recv()

    def to_sibling(d, e):
        chunk = col_chunk(d, e, core)
        source = vec if d == 0 and e == 0 else chunk
        send(source, chunk, ss.at[d, e], sr.at[d, e], sibling)

    def tables(names, prev, last, target_of):
        for c, name in enumerate(names):
            found = jnp.int32(len(names))
            for earlier in range(c):
                found = jnp.where(names[earlier] == name, earlier, found)
            prev[c] = found
        for t in range(16):
            found = jnp.int32(len(names))
            for c, name in enumerate(names):
                found = jnp.where(name == target_of(t), c, found)
            last[t] = found

    mine_row, mine_col = row_chunk(0, 0), col_chunk(0, 0, core)
    send(vec, mine_col, cs.at[0, 1], cr.at[0, 1], far)
    for d in range(1, NY):
        send(vec, mine_row, ys.at[d], yr.at[d], y_peer[d])
    for d in range(1, NX):
        send(vec, mine_col, cs.at[d, 0], cr.at[d, 0], x_peer[d])
    send(vec, mine_row, zs.at[0], zr.at[0], z_peer[NZ // 2])
    for way in WAYS:
        pass_on(way, 0, 0)
    to_sibling(0, 0)

    for s in range(SLOTS):
        pltpu.make_async_copy(tiles.at[0, 0, s], tilebuf.at[s], tsem.at[s]).start()
    for copy in local:
        copy.wait()
    live = cnt[0]
    for s in range(SLOTS):
        rto[0, s] = jnp.where(s < live, br[s], -1)
        cto[0, s] = jnp.where(s < live, bc[s], -1)
    send(cto.at[0], cto.at[1], js.at[0], jr.at[0], sibling)
    for d in range(1, SQ):
        send(rto.at[0], rto.at[d], js.at[d], jr.at[d], y_peer[d])

    for s in range(SLOTS):
        pltpu.make_async_copy(tiles.at[0, 0, s], tilebuf.at[s], tsem.at[s]).wait()

    def turn(s, carry):
        turned[s] = tilebuf[s].T
        return carry

    lax.fori_loop(0, SLOTS, turn, 0)

    for i in range(1, NY):
        chunk = row_chunk(i, 0)
        remote(chunk, chunk, ys.at[i], yr.at[i], y_peer[1]).wait_recv()
        for way in WAYS:
            pass_on(way, 0, i)
    step(0, [0])

    col_wait(0, 1)
    theirs = col_chunk(0, 1, core)
    for d in range(1, NX):
        send(theirs, theirs, cs.at[d, 1], cr.at[d, 1], x_peer[d])
    to_sibling(0, 1)

    chunk = row_chunk(0, NZ // 2)
    remote(chunk, chunk, zs.at[0], zr.at[0], z_peer[1]).wait_recv()
    for d in range(1, NY):
        send(chunk, chunk, us.at[d], ur.at[d], y_peer[d])

    for d in range(1, NX):
        col_wait(d, 0)
        to_sibling(d, 0)
    step(0, range(1, NY))
    step(1, [0])
    for d in range(1, NX):
        col_wait(d, 1)
        to_sibling(d, 1)
    for e in range(NH):
        for d in range(NX):
            chunk = col_chunk(d, e, 1 - core)
            remote(chunk, chunk, ss.at[d, e], sr.at[d, e], sibling).wait_recv()

    def lane_parts(value):
        return [value[:, j * LANES:(j + 1) * LANES] for j in range(LT)]

    def product(pieces, where, blocks, s):
        pair = pieces[where[s] // 2]
        piece = jnp.where(where[s] % 2 == 0, pair[:, :BLK], pair[:, BLK:])
        value = jnp.dot(piece, blocks[s], preferred_element_type=jnp.float32)
        return lane_parts(jnp.where(s < live, value, 0.0))

    def code_chunk(parts, dst, first):
        exponent = exponent_of(most_of(parts))
        inverse = 1.0 / jnp.exp2(exponent)
        for t, part in enumerate(parts):
            dst[first + t] = coded(part, inverse)
        dst[first + len(parts)] = exponent.astype(jnp.int32).astype(jnp.int16)

    def products(pieces, where, blocks, msg, part):
        values = []
        for s in range(part * HALF, (part + 1) * HALF):
            values += product(pieces, where, blocks, s)
        code_chunk(values, msg, 0)

    def combine(groups, prev):
        count = sum(slots for _, slots in groups)
        run[count] = jnp.zeros((LT, VECS, LANES), jnp.float32)
        base = 0
        for msg, slots in groups:
            scale = jnp.exp2(decoded(msg[slots * LT]))
            for s in range(slots):
                before = run[prev[base + s]]
                for j in range(LT):
                    run[base + s, j] = decoded(msg[s * LT + j]) * scale + before[j]
            base += slots

    def block_parts(last, t):
        value = run[last[t]]
        return [value[j] for j in range(LT)]

    for d in range(1, NY):
        code_chunk(product(colbuf, bc, turned, HALF + d), lone.at[d], 0)
        send(lone.at[d], lent.at[d], es.at[d], er.at[d], y_peer[d])
    products(colbuf, bc, turned, ymsg.at[0], 0)
    for d in range(1, SQ):
        send(ymsg.at[0], ymsg.at[d], ps.at[d], pr.at[d], y_peer[d])
    code_chunk(product(colbuf, bc, turned, HALF), lent.at[0], 0)

    step(1, range(1, NY))
    for d in range(1, SQ):
        remote(rto.at[0], rto.at[d], js.at[d], jr.at[d], y_peer[1]).wait_recv()
    full = jnp.int32(0)
    for n in range(1, SQ):
        full = jnp.where(rto[n, HALF] >= 0, n, full)
    for d in range(1, NY):
        remote(lone.at[d], lent.at[d], es.at[d], er.at[d], y_peer[1]).wait_recv()
    kept[0] = lent[full]
    for d in range(1, NY):
        send(kept.at[0], kept.at[d], fs.at[d], fr.at[d], y_peer[d])

    remote(cto.at[0], cto.at[1], js.at[0], jr.at[0], sibling).wait_recv()
    names = [cto[n, s] for n in range(NC) for s in range(SLOTS)]
    tables(names, cprev, clast, lambda t: (t // 2) * 2 * NC + 2 * core + t % 2)
    names = [rto[n, s] for n in range(SQ) for s in range(HALF)]
    names += [rto[full, HALF + (full - m + NY) % NY] for m in range(NY)]
    tables(names, rprev, rlast, lambda t: 2 * col_of(y, 0) + t)

    for i in range(1, NY):
        chunk = row_chunk(i, NZ // 2)
        remote(chunk, chunk, us.at[i], ur.at[i], y_peer[1]).wait_recv()
    for i in range(NY):
        for way in WAYS:
            passed(way, 2, i)

    for part in range(2):
        products(rowbuf, br, tilebuf, cmsg.at[0, part], part)
        send(cmsg.at[0, part], cmsg.at[1, part], ms.at[part], mr.at[part], sibling)

    def chip_parts(xx, e):
        chip = xx * NH + (h + e) % NH
        return block_parts(clast, 2 * chip) + block_parts(clast, 2 * chip + 1)

    for part in range(2):
        remote(cmsg.at[0, part], cmsg.at[1, part], ms.at[part], mr.at[part], sibling).wait_recv()
    combine([(cmsg.at[n, part], HALF) for n in range(NC) for part in range(2)], cprev)
    CH = 2 * LT + 1
    for d in range(1, NX):
        for e in range(NH):
            code_chunk(chip_parts(x_at(d), e), xsend.at[d], e * CH)
        send(xsend.at[d], xrecv.at[d], xs.at[d], xr.at[d], x_peer[d])
    for e in range(NH):
        for t, part in enumerate(chip_parts(x, e)):
            own[e, t] = part

    def place_parts(q):
        first = 2 * z_at(q)
        return block_parts(rlast, first) + block_parts(rlast, first + 1)

    for d in range(1, SQ):
        remote(ymsg.at[0], ymsg.at[d], ps.at[d], pr.at[d], y_peer[1]).wait_recv()
        remote(kept.at[0], kept.at[d], fs.at[d], fr.at[d], y_peer[1]).wait_recv()
    combine([(ymsg.at[n], HALF) for n in range(SQ)] + [(kept.at[m], 1) for m in range(NY)], rprev)
    for q in range(1, PLACES):
        code_chunk(place_parts(q), zsend.at[q], 0)
        send(zsend.at[q], zrecv.at[q], ks.at[q], kr.at[q], z_peer[q])

    def opened(msg, first):
        scale = jnp.exp2(decoded(msg[first + 2 * LT]))
        return [decoded(msg[first + t]) * scale for t in range(2 * LT)]

    for d in range(1, NX):
        remote(xsend.at[d], xrecv.at[d], xs.at[d], xr.at[d], x_peer[1]).wait_recv()

    def with_x(e):
        parts = [own[e, t] for t in range(2 * LT)]
        for d in range(1, NX):
            parts = [a + b for a, b in zip(parts, opened(xrecv.at[d], e * CH))]
        return parts

    code_chunk(with_x(1), hsend, 0)
    send(hsend, hrecv, hs.at[0], hr.at[0], far)
    total = [a + b for a, b in zip(with_x(0), place_parts(0))]
    for q in range(1, PLACES):
        remote(zsend.at[q], zrecv.at[q], ks.at[q], kr.at[q], z_peer[1]).wait_recv()
        total = [a + b for a, b in zip(total, opened(zrecv.at[q], 0))]
    remote(hsend, hrecv, hs.at[0], hr.at[0], far).wait_recv()
    total = [a + b for a, b in zip(total, opened(hrecv, 0))]
    for t, part in enumerate(total):
        out[:, t * LANES:(t + 1) * LANES] = part

    for copy in sent:
        copy.wait_send()


def on_device(vectors, tiles, block_rows, block_cols, counts):
    i16, f32, bf16 = jnp.int16, jnp.float32, jnp.bfloat16
    chunk = 2 * LT + 1
    dma = pltpu.SemaphoreType.DMA

    def smem(shape):
        return pltpu.SMEM(shape, jnp.int32)

    scratch = [
        smem((SLOTS,)), smem((SLOTS,)), smem((1,)),
        smem((SQ, SLOTS)), smem((NC, SLOTS)),
        smem((SQ * HALF + NY,)), smem((16,)),
        smem((NC * SLOTS,)), smem((16,)),
        pltpu.VMEM((NY * NZ, VECS, 2 * BLK), bf16),
        pltpu.VMEM((NX * NH * NC, VECS, 2 * BLK), bf16),
        pltpu.VMEM((SLOTS, BLK, BLK), bf16),
        pltpu.VMEM((SLOTS, BLK, BLK), bf16),
        pltpu.VMEM((SQ, PART, VECS, LANES), i16),
        pltpu.VMEM((NC, 2, PART, VECS, LANES), i16),
        pltpu.VMEM((NY, LONE, VECS, LANES), i16),
        pltpu.VMEM((NY, LONE, VECS, LANES), i16),
        pltpu.VMEM((NY, LONE, VECS, LANES), i16),
        pltpu.VMEM((SQ * HALF + NY + 1, LT, VECS, LANES), f32),
        pltpu.VMEM((PLACES, chunk, VECS, LANES), i16),
        pltpu.VMEM((PLACES, chunk, VECS, LANES), i16),
        pltpu.VMEM((NX, NH * chunk, VECS, LANES), i16),
        pltpu.VMEM((NX, NH * chunk, VECS, LANES), i16),
        pltpu.VMEM((chunk, VECS, LANES), i16),
        pltpu.VMEM((chunk, VECS, LANES), i16),
        pltpu.VMEM((NH, 2 * LT, VECS, LANES), f32),
        dma((3,)), dma((2,)),
        dma((SLOTS,)),
        dma((NY,)), dma((NY,)),
        dma((1,)), dma((1,)),
        dma((2, NZ // 2 - 1, NY)), dma((2, NZ // 2 - 1, NY)),
        dma((NY,)), dma((NY,)),
        dma((NX, NH)), dma((NX, NH)),
        dma((NX, NH)), dma((NX, NH)),
        dma((2,)), dma((2,)),
        dma((PLACES,)), dma((PLACES,)),
        dma((SQ,)), dma((SQ,)),
        dma((NX,)), dma((NX,)),
        dma((1,)), dma((1,)),
        dma((SQ,)), dma((SQ,)),
        dma((NY,)), dma((NY,)),
        dma((NY,)), dma((NY,)),
    ]
    return pl.pallas_call(
        kernel,
        out_shape=jax.ShapeDtypeStruct((VECS, 2 * BLK), f32),
        in_specs=[pl.BlockSpec(memory_space=pltpu.HBM)] * 5,
        out_specs=pl.BlockSpec(memory_space=pltpu.VMEM),
        scratch_shapes=scratch,
        compiler_params=pltpu.CompilerParams(
            collective_id=0, has_side_effects=True, vmem_limit_bytes=64 * 2 ** 20
        ),
    )(vectors, tiles, block_rows, block_cols, counts)


def solution(mesh):
    placed = (
        P(None, ("row", "col")),
        P("row", "col", None, None, None),
        P("row", "col", None),
        P("row", "col", None),
        P("row", "col"),
    )
    return jax.shard_map(
        on_device, mesh=mesh, in_specs=placed, out_specs=P(None, ("row", "col")), check_vma=False
    )
```

```python
import jax
import jax.numpy as jnp
from jax import lax
from jax.experimental import pallas as pl
from jax.experimental.pallas import tpu as pltpu
from jax.sharding import PartitionSpec as P

NX, NH, NC = 4, 2, 2
NY, NZ = 4, 8
VECS, BLK, SLOTS = 16, 512, 8
SQ, PLACES = NY, NZ
WAYS = (1, -1)
LANES = 128
LT = BLK // LANES
HALF = SLOTS // 2
PART = HALF * LT + 1
LONE = LT + 1
MESH = pl.DeviceIdType.MESH
TINY = 2.0 ** -110


def exponent_of(most):
    return jnp.ceil(jnp.log2(jnp.maximum(most, TINY)) - 14.98)


def coded(values, inverse):
    return jnp.round(values * inverse).astype(jnp.int32).astype(jnp.int16)


def decoded(code):
    return code.astype(jnp.int32).astype(jnp.float32)


def most_of(parts):
    most = jnp.abs(parts[0])
    for part in parts[1:]:
        most = jnp.maximum(most, jnp.abs(part))
    return most


def kernel(
    vec, tiles, br_hbm, bc_hbm, cnt_hbm, out,
    br, bc, cnt, rto, cto, rprev, rlast, cprev, clast,
    rowbuf, colbuf, tilebuf, turned, ymsg, cmsg, lone, lent, kept, run,
    zsend, zrecv, xsend, xrecv, hsend, hrecv, own,
    isem, vsem, tsem, ys, yr, zs, zr, qs, qr, us, ur, cs, cr, ss, sr, ms, mr, ks, kr, ps, pr, xs, xr, hs, hr, js, jr, es, er, fs, fr,
):
    me_r, me_c = lax.axis_index("row"), lax.axis_index("col")
    x, h, core = me_r // (NH * NC), (me_r // NC) % NH, me_r % NC
    y, z = me_c // NZ, me_c % NZ

    def row_of(xx, hh, cc):
        return (xx * NH + hh) * NC + cc

    def col_of(yy, zz):
        return yy * NZ + zz

    def y_at(d):
        return (y + d + NY) % NY

    def z_at(d):
        return (z + d + NZ) % NZ

    def x_at(d):
        return (x + d + NX) % NX

    sibling = (row_of(x, h, 1 - core), me_c)
    far = (row_of(x, 1 - h, core), me_c)
    x_peer = [None] + [(row_of(x_at(d), h, core), me_c) for d in range(1, NX)]
    y_peer = [None] + [(me_r, col_of(y_at(d), z)) for d in range(1, NY)]
    z_peer = [None] + [(me_r, col_of(y, z_at(d))) for d in range(1, NZ)]

    def remote(src, dst, send, recv, device):
        return pltpu.make_async_remote_copy(
            src_ref=src, dst_ref=dst, send_sem=send, recv_sem=recv,
            device_id=device, device_id_type=MESH,
        )

    sent = []

    def send(*args):
        copy = remote(*args)
        copy.start()
        sent.append(copy)

    barrier = pltpu.get_barrier_semaphore()
    partners = [sibling, far] + x_peer[1:] + y_peer[1:] + [z_peer[1], z_peer[4], z_peer[7]]
    for device in partners:
        pl.semaphore_signal(barrier, inc=1, device_id=device, device_id_type=MESH)

    local = [
        pltpu.make_async_copy(br_hbm.at[0, 0], br, isem.at[0]),
        pltpu.make_async_copy(bc_hbm.at[0, 0], bc, isem.at[1]),
        pltpu.make_async_copy(cnt_hbm.at[0], cnt, isem.at[2]),
        pltpu.make_async_copy(vec, rowbuf.at[me_c], vsem.at[0]),
        pltpu.make_async_copy(vec, colbuf.at[me_r], vsem.at[1]),
    ]
    for copy in local:
        copy.start()
    pl.semaphore_wait(barrier, len(partners))

    def row_chunk(dy, dz):
        return rowbuf.at[col_of(y_at(-dy), z_at(-dz))]

    def col_chunk(d, e, cc):
        return colbuf.at[row_of(x_at(-d), (h + e) % NH, cc)]

    def col_piece(ref, e, k):
        return ref.at[:, pl.ds(k * BLK, BLK)] if e else ref

    def pass_on(way, hop, i):
        chunk = row_chunk(i, way * hop)
        source = vec if hop == 0 and i == 0 else chunk
        w = WAYS.index(way)
        send(source, chunk, qs.at[w, hop, i], qr.at[w, hop, i], z_peer[way % NZ])

    def passed(way, hop, i):
        chunk = row_chunk(i, way * (hop + 1))
        w = WAYS.index(way)
        remote(chunk, chunk, qs.at[w, hop, i], qr.at[w, hop, i], z_peer[1]).wait_recv()

    def step(hop, group):
        for i in group:
            for way in WAYS:
                passed(way, hop, i)
                pass_on(way, hop + 1, i)

    def col_wait(d, e, k):
        chunk = col_piece(col_chunk(d, e, core), e, k)
        remote(chunk, chunk, cs.at[d, e, k], cr.at[d, e, k], far).wait_recv()

    def to_sibling(d, e, k):
        chunk = col_piece(col_chunk(d, e, core), e, k)
        source = vec if d == 0 and e == 0 else chunk
        send(source, chunk, ss.at[d, e, k], sr.at[d, e, k], sibling)

    def tables(names, prev, last, target_of):
        for c, name in enumerate(names):
            found = jnp.int32(len(names))
            for earlier in range(c):
                found = jnp.where(names[earlier] == name, earlier, found)
            prev[c] = found
        for t in range(16):
            found = jnp.int32(len(names))
            for c, name in enumerate(names):
                found = jnp.where(name == target_of(t), c, found)
            last[t] = found

    mine_row, mine_col = row_chunk(0, 0), col_chunk(0, 0, core)
    for k in range(2):
        send(col_piece(vec, 1, k), col_piece(mine_col, 1, k), cs.at[0, 1, k], cr.at[0, 1, k], far)
    for d in range(1, NY):
        send(vec, mine_row, ys.at[d], yr.at[d], y_peer[d])
    for d in range(1, NX):
        send(vec, mine_col, cs.at[d, 0, 0], cr.at[d, 0, 0], x_peer[d])
    send(vec, mine_row, zs.at[0], zr.at[0], z_peer[NZ // 2])
    for way in WAYS:
        pass_on(way, 0, 0)
    to_sibling(0, 0, 0)

    for s in range(SLOTS):
        pltpu.make_async_copy(tiles.at[0, 0, s], tilebuf.at[s], tsem.at[s]).start()
    for copy in local:
        copy.wait()
    live = cnt[0]
    for s in range(SLOTS):
        rto[0, s] = jnp.where(s < live, br[s], -1)
        cto[0, s] = jnp.where(s < live, bc[s], -1)
    send(cto.at[0], cto.at[1], js.at[0], jr.at[0], sibling)
    for d in range(1, SQ):
        send(rto.at[0], rto.at[d], js.at[d], jr.at[d], y_peer[d])

    for s in range(SLOTS):
        pltpu.make_async_copy(tiles.at[0, 0, s], tilebuf.at[s], tsem.at[s]).wait()

    def turn(s, carry):
        turned[s] = tilebuf[s].T
        return carry

    lax.fori_loop(0, SLOTS, turn, 0)

    for i in range(1, NY):
        chunk = row_chunk(i, 0)
        remote(chunk, chunk, ys.at[i], yr.at[i], y_peer[1]).wait_recv()
        for way in WAYS:
            pass_on(way, 0, i)
    step(0, [0])

    for k in range(2):
        col_wait(0, 1, k)
        theirs = col_piece(col_chunk(0, 1, core), 1, k)
        for d in range(1, NX):
            send(theirs, theirs, cs.at[d, 1, k], cr.at[d, 1, k], x_peer[d])
        to_sibling(0, 1, k)

    chunk = row_chunk(0, NZ // 2)
    remote(chunk, chunk, zs.at[0], zr.at[0], z_peer[1]).wait_recv()
    for d in range(1, NY):
        send(chunk, chunk, us.at[d], ur.at[d], y_peer[d])

    for d in range(1, NX):
        col_wait(d, 0, 0)
        to_sibling(d, 0, 0)
    step(0, range(1, NY))
    step(1, [0])
    for k in range(2):
        for d in range(1, NX):
            col_wait(d, 1, k)
            to_sibling(d, 1, k)
    for e in range(NH):
        for d in range(NX):
            for k in range(1 + e):
                chunk = col_piece(col_chunk(d, e, 1 - core), e, k)
                remote(chunk, chunk, ss.at[d, e, k], sr.at[d, e, k], sibling).wait_recv()

    def lane_parts(value):
        return [value[:, j * LANES:(j + 1) * LANES] for j in range(LT)]

    def product(pieces, where, blocks, s):
        pair = pieces[where[s] // 2]
        piece = jnp.where(where[s] % 2 == 0, pair[:, :BLK], pair[:, BLK:])
        value = jnp.dot(piece, blocks[s], preferred_element_type=jnp.float32)
        return lane_parts(jnp.where(s < live, value, 0.0))

    def code_chunk(parts, dst, first):
        exponent = exponent_of(most_of(parts))
        inverse = 1.0 / jnp.exp2(exponent)
        for t, part in enumerate(parts):
            dst[first + t] = coded(part, inverse)
        dst[first + len(parts)] = exponent.astype(jnp.int32).astype(jnp.int16)

    def products(pieces, where, blocks, msg, part):
        values = []
        for s in range(part * HALF, (part + 1) * HALF):
            values += product(pieces, where, blocks, s)
        code_chunk(values, msg, 0)

    def combine(groups, prev, base, count):
        if base == 0:
            run[count] = jnp.zeros((LT, VECS, LANES), jnp.float32)
        for msg, slots in groups:
            scale = jnp.exp2(decoded(msg[slots * LT]))
            for s in range(slots):
                before = run[prev[base + s]]
                for j in range(LT):
                    run[base + s, j] = decoded(msg[s * LT + j]) * scale + before[j]
            base += slots

    def block_parts(last, t):
        value = run[last[t]]
        return [value[j] for j in range(LT)]

    for d in range(1, NY):
        code_chunk(product(colbuf, bc, turned, HALF + d), lone.at[d], 0)
        send(lone.at[d], lent.at[d], es.at[d], er.at[d], y_peer[d])
    products(colbuf, bc, turned, ymsg.at[0], 0)
    for d in range(1, SQ):
        send(ymsg.at[0], ymsg.at[d], ps.at[d], pr.at[d], y_peer[d])
    code_chunk(product(colbuf, bc, turned, HALF), lent.at[0], 0)

    step(1, range(1, NY))
    for d in range(1, SQ):
        remote(rto.at[0], rto.at[d], js.at[d], jr.at[d], y_peer[1]).wait_recv()
    full = jnp.int32(0)
    for n in range(1, SQ):
        full = jnp.where(rto[n, HALF] >= 0, n, full)
    for d in range(1, NY):
        remote(lone.at[d], lent.at[d], es.at[d], er.at[d], y_peer[1]).wait_recv()
    kept[0] = lent[full]
    for d in range(1, NY):
        send(kept.at[0], kept.at[d], fs.at[d], fr.at[d], y_peer[d])

    remote(cto.at[0], cto.at[1], js.at[0], jr.at[0], sibling).wait_recv()
    names = [cto[n, s] for n in range(NC) for s in range(SLOTS)]
    tables(names, cprev, clast, lambda t: (t // 2) * 2 * NC + 2 * core + t % 2)
    names = [rto[n, s] for n in range(SQ) for s in range(HALF)]
    names += [rto[full, HALF + (full - m + NY) % NY] for m in range(NY)]
    tables(names, rprev, rlast, lambda t: 2 * col_of(y, 0) + t)

    for i in range(1, NY):
        chunk = row_chunk(i, NZ // 2)
        remote(chunk, chunk, us.at[i], ur.at[i], y_peer[1]).wait_recv()
    for i in range(NY):
        for way in WAYS:
            passed(way, 2, i)

    for part in range(2):
        products(rowbuf, br, tilebuf, cmsg.at[0, part], part)
        send(cmsg.at[0, part], cmsg.at[1, part], ms.at[part], mr.at[part], sibling)

    def chip_parts(xx, e):
        chip = xx * NH + (h + e) % NH
        return block_parts(clast, 2 * chip) + block_parts(clast, 2 * chip + 1)

    for part in range(2):
        remote(cmsg.at[0, part], cmsg.at[1, part], ms.at[part], mr.at[part], sibling).wait_recv()
    combine([(cmsg.at[n, part], HALF) for n in range(NC) for part in range(2)], cprev, 0, NC * SLOTS)
    CH = 2 * LT + 1
    for d in range(1, NX):
        for e in range(NH):
            code_chunk(chip_parts(x_at(d), e), xsend.at[d], e * CH)
        send(xsend.at[d], xrecv.at[d], xs.at[d], xr.at[d], x_peer[d])
    for e in range(NH):
        for t, part in enumerate(chip_parts(x, e)):
            own[e, t] = part

    def place_parts(q):
        first = 2 * z_at(q)
        return block_parts(rlast, first) + block_parts(rlast, first + 1)

    count = SQ * HALF + NY
    for d in range(1, SQ):
        remote(ymsg.at[0], ymsg.at[d], ps.at[d], pr.at[d], y_peer[1]).wait_recv()
    combine([(ymsg.at[n], HALF) for n in range(SQ)], rprev, 0, count)
    for d in range(1, NY):
        remote(kept.at[0], kept.at[d], fs.at[d], fr.at[d], y_peer[1]).wait_recv()
    combine([(kept.at[m], 1) for m in range(NY)], rprev, SQ * HALF, count)
    for q in range(1, PLACES):
        code_chunk(place_parts(q), zsend.at[q], 0)
        send(zsend.at[q], zrecv.at[q], ks.at[q], kr.at[q], z_peer[q])

    def opened(msg, first):
        scale = jnp.exp2(decoded(msg[first + 2 * LT]))
        return [decoded(msg[first + t]) * scale for t in range(2 * LT)]

    for d in range(1, NX):
        remote(xsend.at[d], xrecv.at[d], xs.at[d], xr.at[d], x_peer[1]).wait_recv()

    def with_x(e):
        parts = [own[e, t] for t in range(2 * LT)]
        for d in range(1, NX):
            parts = [a + b for a, b in zip(parts, opened(xrecv.at[d], e * CH))]
        return parts

    code_chunk(with_x(1), hsend, 0)
    send(hsend, hrecv, hs.at[0], hr.at[0], far)
    total = [a + b for a, b in zip(with_x(0), place_parts(0))]
    for q in range(1, PLACES):
        remote(zsend.at[q], zrecv.at[q], ks.at[q], kr.at[q], z_peer[1]).wait_recv()
        total = [a + b for a, b in zip(total, opened(zrecv.at[q], 0))]
    remote(hsend, hrecv, hs.at[0], hr.at[0], far).wait_recv()
    total = [a + b for a, b in zip(total, opened(hrecv, 0))]
    for t, part in enumerate(total):
        out[:, t * LANES:(t + 1) * LANES] = part

    for copy in sent:
        copy.wait_send()


def on_device(vectors, tiles, block_rows, block_cols, counts):
    i16, f32, bf16 = jnp.int16, jnp.float32, jnp.bfloat16
    chunk = 2 * LT + 1
    dma = pltpu.SemaphoreType.DMA

    def smem(shape):
        return pltpu.SMEM(shape, jnp.int32)

    scratch = [
        smem((SLOTS,)), smem((SLOTS,)), smem((1,)),
        smem((SQ, SLOTS)), smem((NC, SLOTS)),
        smem((SQ * HALF + NY,)), smem((16,)),
        smem((NC * SLOTS,)), smem((16,)),
        pltpu.VMEM((NY * NZ, VECS, 2 * BLK), bf16),
        pltpu.VMEM((NX * NH * NC, VECS, 2 * BLK), bf16),
        pltpu.VMEM((SLOTS, BLK, BLK), bf16),
        pltpu.VMEM((SLOTS, BLK, BLK), bf16),
        pltpu.VMEM((SQ, PART, VECS, LANES), i16),
        pltpu.VMEM((NC, 2, PART, VECS, LANES), i16),
        pltpu.VMEM((NY, LONE, VECS, LANES), i16),
        pltpu.VMEM((NY, LONE, VECS, LANES), i16),
        pltpu.VMEM((NY, LONE, VECS, LANES), i16),
        pltpu.VMEM((SQ * HALF + NY + 1, LT, VECS, LANES), f32),
        pltpu.VMEM((PLACES, chunk, VECS, LANES), i16),
        pltpu.VMEM((PLACES, chunk, VECS, LANES), i16),
        pltpu.VMEM((NX, NH * chunk, VECS, LANES), i16),
        pltpu.VMEM((NX, NH * chunk, VECS, LANES), i16),
        pltpu.VMEM((chunk, VECS, LANES), i16),
        pltpu.VMEM((chunk, VECS, LANES), i16),
        pltpu.VMEM((NH, 2 * LT, VECS, LANES), f32),
        dma((3,)), dma((2,)),
        dma((SLOTS,)),
        dma((NY,)), dma((NY,)),
        dma((1,)), dma((1,)),
        dma((2, NZ // 2 - 1, NY)), dma((2, NZ // 2 - 1, NY)),
        dma((NY,)), dma((NY,)),
        dma((NX, NH, 2)), dma((NX, NH, 2)),
        dma((NX, NH, 2)), dma((NX, NH, 2)),
        dma((2,)), dma((2,)),
        dma((PLACES,)), dma((PLACES,)),
        dma((SQ,)), dma((SQ,)),
        dma((NX,)), dma((NX,)),
        dma((1,)), dma((1,)),
        dma((SQ,)), dma((SQ,)),
        dma((NY,)), dma((NY,)),
        dma((NY,)), dma((NY,)),
    ]
    return pl.pallas_call(
        kernel,
        out_shape=jax.ShapeDtypeStruct((VECS, 2 * BLK), f32),
        in_specs=[pl.BlockSpec(memory_space=pltpu.HBM)] * 5,
        out_specs=pl.BlockSpec(memory_space=pltpu.VMEM),
        scratch_shapes=scratch,
        compiler_params=pltpu.CompilerParams(
            collective_id=0, has_side_effects=True, vmem_limit_bytes=64 * 2 ** 20
        ),
    )(vectors, tiles, block_rows, block_cols, counts)


def solution(mesh):
    placed = (
        P(None, ("row", "col")),
        P("row", "col", None, None, None),
        P("row", "col", None),
        P("row", "col", None),
        P("row", "col"),
    )
    return jax.shard_map(
        on_device, mesh=mesh, in_specs=placed, out_specs=P(None, ("row", "col")), check_vma=False
    )
```
